32 devices in a mesh: row: 4 (over x, core), col: 8 (over z, y).
Axes of the slice: x: 2, y: 2, z: 4, core: 2. Of those that a mesh axis runs over, the one named last changes fastest.
Arguments:
- tokens: bfloat16 [4096, 16384], P('row', 'col'), may hold values from -6 to 6
- up_weight: bfloat16 [16384, 28672], P('row', 'col'), may hold values from -0.0625 to 0.0625
Outputs:
- projected: bfloat16 [4096, 28672], P('row', 'col')
The draws below stay inside these ranges and needn't reach their ends.
All inputs are finite; a program needn't handle non-finite values.
Results may differ from the reference program's by a relative error of at most 0.001.
Values may be sent and summed in bfloat16 or wider, within the bound.
No kernel may reach another device: no remote copies, remote signals or barrier semaphores. Data moves between devices by JAX's collectives and lax.ppermute only.
A program may use at most 192 MiB of HBM per device.

```python
import jax
import jax.numpy as jnp
from jax import lax

D = 16384
FF = 28672
TB = 1024
TOKENS = 4096
BAND = 8192
N_ROW = 4


def levels(rng, extent, split, smallest, largest):
    loudness = 1.0
    for axis_at, parts in split:
        heights = jax.random.uniform(jax.random.fold_in(jax.random.fold_in(rng, 6), axis_at), (parts,), jnp.float32, smallest / len(split), largest / len(split))
        loudness = loudness * jnp.repeat(jnp.exp(heights), extent[axis_at] // parts).reshape((-1,) + (1,) * (len(extent) - 1 - axis_at))
    return loudness


def scatter_about(stream_key, extent, deviation, reach, split=(), held_as=jnp.bfloat16):
    array = deviation * jax.random.normal(stream_key, extent, jnp.float32)
    if split:
        array = array * levels(stream_key, extent, split, -0.22, 0.18)
    return jnp.clip(array, -reach, reach).astype(held_as)


def setup_inputs(seed: int = 0) -> dict:
    key_list = jax.random.split(jax.random.key(seed), 3)
    return {
        "tokens": scatter_about(key_list[0], (TOKENS, D), 1.0, 6.0, ((0, 4), (1, 8))),
        "up_weight": scatter_about(key_list[1], (D, FF), BAND ** -0.5, 0.0625, ((0, 4), (1, 8))),
    }


def reference(tokens, up_weight):
    height = D // N_ROW

    def one_group(group):
        token_block = lax.dynamic_slice_in_dim(tokens, group * TB, TB, 0)
        following = (group + 1) % N_ROW
        first_part = jnp.dot(lax.dynamic_slice_in_dim(token_block, group * height, height, 1),
                             lax.dynamic_slice_in_dim(up_weight, group * height, height, 0),
                             preferred_element_type=jnp.float32)
        second_part = jnp.dot(lax.dynamic_slice_in_dim(token_block, following * height, height, 1),
                              lax.dynamic_slice_in_dim(up_weight, following * height, height, 0),
                              preferred_element_type=jnp.float32)
        return (first_part + second_part).astype(jnp.bfloat16)

    stacked = lax.map(one_group, jnp.arange(N_ROW, dtype=jnp.int32))
    return stacked.reshape(TOKENS, FF)
```

```python
import functools

import jax
import jax.numpy as jnp
from jax import lax
from jax.experimental import pallas as pl
from jax.experimental.pallas import tpu as pltpu
from jax.sharding import PartitionSpec as P

AXES = ("row", "col")
PIECES = 8
STREAM = (0, 1, 1, 1, 0, 1, 1, 1, 0, 1, 1, 0, 0, 0, 0, 0)
SUB = 2
BACK_STEPS = 3
MIB = 1024 * 1024
CHOOSE_VMEM = 4 * MIB
PRODUCT_VMEM = 12 * MIB
ANYWHERE = pl.BlockSpec(memory_space=pl.ANY)
NO_COST = pl.CostEstimate(flops=0, bytes_accessed=0, transcendentals=0)
TOKEN = jax.ShapeDtypeStruct((8, 128), jnp.float32)


def through(sources, scratch, out, sems):
    if len(sources) == 1:
        half = out.shape[0] // 2
        sources = [sources[0].at[pl.ds(0, half)], sources[0].at[pl.ds(half, half)]]
    inward, outward, at = [], [], 0
    for i, source in enumerate(sources):
        rows = pl.ds(at, source.shape[0])
        inward.append(pltpu.make_async_copy(source, scratch.at[rows], sems.at[2 * i]))
        outward.append(pltpu.make_async_copy(scratch.at[rows], out.at[rows], sems.at[2 * i + 1]))
        at += source.shape[0]
    for c in inward:
        c.start()
    for i, c in enumerate(outward):
        inward[i].wait()
        c.start()
    for c in outward:
        c.wait()


def choose_kernel(options, parts, which_of, start, size, *refs):
    out, _, scratch, sems = refs[-4:]
    index = which_of(lax.axis_index("row"), lax.axis_index("col"))
    for value in range(options):
        sources = refs[value * parts:(value + 1) * parts]
        if parts == 1 and sources[0].shape[0] != size:
            sources = [sources[0].at[pl.ds(start, size)]]

        @pl.when(index == value)
        def _(sources=sources):
            through(sources, scratch, out, sems)


def choose(which_of, options, start, size, tokens, into=None):
    parts = len(options[0])
    width, dtype = options[0][0].shape[1], options[0][0].dtype
    args = [a for option in options for a in option] + list(tokens)
    aliases = {}
    if into is not None:
        aliases = {len(args): 0}
        args.append(into)
    return pl.pallas_call(
        functools.partial(choose_kernel, len(options), parts, which_of, start, size),
        out_shape=(jax.ShapeDtypeStruct((size, width), dtype), TOKEN),
        in_specs=[ANYWHERE] * len(args),
        out_specs=(ANYWHERE, ANYWHERE),
        scratch_shapes=[pltpu.VMEM((size, width), dtype), pltpu.SemaphoreType.DMA((2 * max(parts, 2),))],
        input_output_aliases=aliases,
        compiler_params=pltpu.CompilerParams(vmem_limit_bytes=CHOOSE_VMEM),
        cost_estimate=NO_COST,
    )(*args)


def load_kernel(x, *refs):
    out, _, sem = refs[-3:]
    copy = pltpu.make_async_copy(x, out, sem)
    copy.start()
    copy.wait()


def load(x, tokens):
    return pl.pallas_call(
        load_kernel,
        out_shape=(pltpu.VMEM(x.shape, x.dtype), TOKEN),
        in_specs=[ANYWHERE] * (1 + len(tokens)),
        out_specs=(pl.BlockSpec(memory_space=pltpu.VMEM), ANYWHERE),
        scratch_shapes=[pltpu.SemaphoreType.DMA],
        compiler_params=pltpu.CompilerParams(vmem_limit_bytes=MIB),
        cost_estimate=NO_COST,
    )(pltpu.with_memory_space_constraint(x, pltpu.HBM), *tokens)


def gate_kernel(*refs):
    del refs


def gate(x, tokens):
    return pl.pallas_call(
        gate_kernel,
        out_shape=(jax.ShapeDtypeStruct(x.shape, x.dtype), TOKEN),
        in_specs=[ANYWHERE] * (1 + len(tokens)),
        out_specs=(ANYWHERE, ANYWHERE),
        input_output_aliases={0: 0},
        compiler_params=pltpu.CompilerParams(vmem_limit_bytes=MIB),
        cost_estimate=NO_COST,
    )(x, *tokens)


def product_kernel(start, has_back, tile, side_of, mine, other, weight, *refs):
    if has_back:
        back = refs[0]
        out, _, near, far, slots, in_sems, out_sems, held, back_sems = refs[-9:]
    else:
        out, _, near, far, slots, in_sems, out_sems = refs[-7:]
    many, half = near.shape
    tiles = weight.shape[1] // tile

    def back_copy(j, at):
        return pltpu.make_async_copy(back.at[:, pl.ds(at, tile)], held.at[:, pl.ds(at, tile)], back_sems.at[j])

    def out_copy(j, slot):
        at = pl.multiple_of(j * tile, tile)
        return pltpu.make_async_copy(slots.at[slot], out.at[pl.ds(start, many), pl.ds(at, tile)], out_sems.at[slot])

    fetch = [pltpu.make_async_copy(mine, near, in_sems.at[0]), pltpu.make_async_copy(other, far, in_sems.at[1])]
    for c in fetch:
        c.start()
    if has_back:
        for j in range(tiles):
            back_copy(j, j * tile).start()
    for c in fetch:
        c.wait()
    side = side_of(lax.axis_index("col"))
    near_rows = pl.ds(pl.multiple_of(side * half, half), half)
    far_rows = pl.ds(pl.multiple_of((1 - side) * half, half), half)

    def one_tile(j, carry):
        slot = lax.rem(j, 2)
        at = pl.multiple_of(j * tile, tile)
        total = jnp.dot(near[...], weight[near_rows, pl.ds(at, tile)], preferred_element_type=jnp.float32)
        total += jnp.dot(far[...], weight[far_rows, pl.ds(at, tile)], preferred_element_type=jnp.float32)
        if has_back:
            back_copy(j, at).wait()
            total += held[:, pl.ds(at, tile)]
        pl.when(j >= 2)(lambda: out_copy(j - 2, slot).wait())
        slots[slot] = total.astype(out.dtype)
        out_copy(j, slot).start()
        return carry

    lax.fori_loop(0, tiles, one_tile, 0)
    for j in range(max(0, tiles - 2), tiles):
        out_copy(j, j % 2).wait()


def product(side_of, mine, other, weight, tokens, back=None, into=None, start=0):
    depth, width = weight.shape
    many = mine.shape[0]
    tile = max(t for t in range(128, 513, 128) if width % t == 0)
    args = [mine, other, pltpu.with_memory_space_constraint(weight, pltpu.VMEM)]
    in_specs = [ANYWHERE, ANYWHERE, pl.BlockSpec(memory_space=pltpu.VMEM)]
    aliases = {}
    dtype = jnp.float32 if back is None else jnp.bfloat16
    scratch = [
        pltpu.VMEM((many, depth // 2), weight.dtype),
        pltpu.VMEM((many, depth // 2), weight.dtype),
        pltpu.VMEM((2, many, tile), dtype),
        pltpu.SemaphoreType.DMA((2,)),
        pltpu.SemaphoreType.DMA((2,)),
    ]
    total = many
    if back is not None:
        total = into[0]
        in_specs.append(ANYWHERE)
        args.append(back)
        scratch += [pltpu.VMEM((many, width), jnp.float32), pltpu.SemaphoreType.DMA((width // tile,))]
        if into[1] is not None:
            aliases = {len(args): 0}
            in_specs.append(ANYWHERE)
            args.append(into[1])
    in_specs += [ANYWHERE] * len(tokens)
    args += tokens
    return pl.pallas_call(
        functools.partial(product_kernel, start, back is not None, tile, side_of),
        out_shape=(jax.ShapeDtypeStruct((total, width), dtype), TOKEN),
        in_specs=in_specs,
        out_specs=(ANYWHERE, ANYWHERE),
        scratch_shapes=scratch,
        input_output_aliases=aliases,
        compiler_params=pltpu.CompilerParams(vmem_limit_bytes=PRODUCT_VMEM),
        cost_estimate=pl.CostEstimate(flops=4 * many * depth * width, bytes_accessed=0, transcendentals=0),
    )(*args)


def body(n_row, n_col, tokens, weight):
    inner = n_col // n_row
    assert inner == 2
    count = tokens.shape[0]
    size = count // PIECES

    def device(r, b, s):
        return (r % n_row) * n_col + (b % n_row) * inner + s

    sides = range(inner)
    chain = [(device(r, r - d, s), device(r, r - d - 1, s)) for r in range(n_row) for d in range(n_row - 1) for s in sides]
    chain += [(device(r - 1, r, s), device(r, r, s)) for r in range(n_row) for s in sides]
    everyone = [(r, b, s) for r in range(n_row) for b in range(n_row) for s in sides]
    swap_pairs = [(device(r, b, s), device(r, b, 1 - s)) for r, b, s in everyone]
    back_pairs = [(device(r, b, s), device(r - 1, b, s)) for r, b, s in everyone]

    def block_of(col):
        return lax.div(col, inner)

    def side_of(col):
        return lax.rem(col, inner)

    def distance(row, col):
        return lax.rem(row - block_of(col) + n_row, n_row)

    def crosses(row, col):
        return jnp.where(lax.rem(row + 1, n_row) == block_of(col), 0, 1)

    def sends(row, col):
        return jnp.where(row == block_of(col), 0, -1)

    tokens = pltpu.with_memory_space_constraint(tokens, pltpu.HBM)
    counts = [0, 0]
    pieces = []
    for group in STREAM:
        pieces.append((group, counts[group]))
        counts[group] += 1
    total = len(pieces)
    chunk = size // SUB
    chunks = total * SUB
    whole = SUB * (n_row + 1) - 1
    when = {at: at * SUB + whole + SUB for at, (group, _) in enumerate(pieces) if group == 1}
    sent_back = []
    for at in sorted(when):
        sent_back.append(max([when[at] + 1] + [b + BACK_STEPS for b in sent_back[-1:]]))
    for at, (group, piece) in enumerate(pieces):
        if group == 0:
            step = max(at * SUB + whole + SUB, sent_back[piece] + BACK_STEPS + 1)
            while step in when.values() or (step - whole) % SUB and step < chunks - SUB:
                step += 1
            when[at] = step

    def rows_of(k):
        return pieces[k // SUB][1] * size + k % SUB * chunk

    seen = []
    sent, held_last, mine, other, back, arriving = {}, {}, {}, {}, {}, {}
    out, waiting = None, []
    last_chain = chunks - 1 + SUB * (n_row - 1)
    first = 0 if pieces[0][0] == 1 else SUB
    for step in range(first, max(when.values()) + 1):
        if step <= last_chain + SUB:
            value, token = arriving.pop(step - SUB, None), None
            came = value
            if step < chunks and pieces[step // SUB][0] == 1:
                options = [[tokens]] if value is None else [[tokens], [value]]
                value, token = choose(crosses, options, rows_of(step), chunk, seen)
                seen = [token]
            else:
                came = None
            if 0 <= step - SUB < chunks and pieces[step // SUB - 1][0] == 0:
                value, token = choose(sends, [[tokens]], rows_of(step - SUB), chunk, seen, value)
                seen = [token]
            if token is None:
                value, token = gate(value, seen)
                seen = [token]
            sent[step] = value
            held_last[step] = value if came is None else came
            if step <= last_chain:
                with jax.named_scope(f"chain{step}"):
                    arriving[step] = lax.ppermute(value, AXES, chain)
        if step == first + SUB - 1:
            weight, token = load(weight, seen)
            seen = [token]
        if waiting and step >= sent_back[waiting[0][0]]:
            piece, partial = waiting.pop(0)
            if piece > 1:
                back[piece - 2], token = gate(back[piece - 2], seen)
                seen = [token]
            partial, token = gate(partial, seen)
            seen = [token]
            with jax.named_scope(f"back{piece}"):
                back[piece] = lax.ppermute(partial, AXES, back_pairs)
        at, part = divmod(step - whole, SUB)
        if part == 0 and 0 <= at < total:
            held = [sent] * (n_row - 1) + [held_last]
            options = [[held[d][(at + 1 + d) * SUB + k] for k in range(SUB)] for d in range(n_row)]
            mine[at], token = choose(distance, options, 0, size, seen)
            seen = [token]
            with jax.named_scope(f"swap{at}"):
                other[at] = lax.ppermute(mine[at], AXES, swap_pairs)
        for at in range(total):
            if when[at] != step:
                continue
            group, piece = pieces[at]
            if group == 1:
                partial, token = product(side_of, mine[at], other[at], weight, seen)
                seen = [token]
                waiting.append((piece, partial))
            else:
                out, token = product(
                    side_of, mine[at], other[at], weight, seen, back[piece], (count, out), piece * size
                )
                seen = [token]
    return out


def solution(mesh):
    n_row, n_col = mesh.shape["row"], mesh.shape["col"]
    placed = P("row", "col")
    return jax.shard_map(
        functools.partial(body, n_row, n_col), mesh=mesh, in_specs=(placed, placed), out_specs=placed, check_vma=False
    )
```

```python
import functools

import jax
import jax.numpy as jnp
from jax import lax
from jax.experimental import pallas as pl
from jax.experimental.pallas import tpu as pltpu
from jax.sharding import PartitionSpec as P

AXES = ("row", "col")
PIECES = 8
STREAM = (0, 1, 1, 1, 1, 1, 1, 1, 1, 0, 0, 0, 0, 0, 0, 0)
SUB = 2
BACK_STEPS = 3
MIB = 1024 * 1024
CHOOSE_VMEM = 4 * MIB
PRODUCT_VMEM = 12 * MIB
ANYWHERE = pl.BlockSpec(memory_space=pl.ANY)
NO_COST = pl.CostEstimate(flops=0, bytes_accessed=0, transcendentals=0)
TOKEN = jax.ShapeDtypeStruct((8, 128), jnp.float32)


def through(sources, scratch, out, sems):
    if len(sources) == 1:
        half = out.shape[0] // 2
        sources = [sources[0].at[pl.ds(0, half)], sources[0].at[pl.ds(half, half)]]
    inward, outward, at = [], [], 0
    for i, source in enumerate(sources):
        rows = pl.ds(at, source.shape[0])
        inward.append(pltpu.make_async_copy(source, scratch.at[rows], sems.at[2 * i]))
        outward.append(pltpu.make_async_copy(scratch.at[rows], out.at[rows], sems.at[2 * i + 1]))
        at += source.shape[0]
    for c in inward:
        c.start()
    for i, c in enumerate(outward):
        inward[i].wait()
        c.start()
    for c in outward:
        c.wait()


def choose_kernel(options, parts, which_of, start, size, *refs):
    out, _, scratch, sems = refs[-4:]
    index = which_of(lax.axis_index("row"), lax.axis_index("col"))
    for value in range(options):
        sources = refs[value * parts:(value + 1) * parts]
        if parts == 1 and sources[0].shape[0] != size:
            sources = [sources[0].at[pl.ds(start, size)]]

        @pl.when(index == value)
        def _(sources=sources):
            through(sources, scratch, out, sems)


def choose(which_of, options, start, size, tokens, into=None):
    parts = len(options[0])
    width, dtype = options[0][0].shape[1], options[0][0].dtype
    args = [a for option in options for a in option] + list(tokens)
    aliases = {}
    if into is not None:
        aliases = {len(args): 0}
        args.append(into)
    return pl.pallas_call(
        functools.partial(choose_kernel, len(options), parts, which_of, start, size),
        out_shape=(jax.ShapeDtypeStruct((size, width), dtype), TOKEN),
        in_specs=[ANYWHERE] * len(args),
        out_specs=(ANYWHERE, ANYWHERE),
        scratch_shapes=[pltpu.VMEM((size, width), dtype), pltpu.SemaphoreType.DMA((2 * max(parts, 2),))],
        input_output_aliases=aliases,
        compiler_params=pltpu.CompilerParams(vmem_limit_bytes=CHOOSE_VMEM),
        cost_estimate=NO_COST,
    )(*args)


def load_kernel(x, *refs):
    out, _, sem = refs[-3:]
    copy = pltpu.make_async_copy(x, out, sem)
    copy.start()
    copy.wait()


def load(x, tokens):
    return pl.pallas_call(
        load_kernel,
        out_shape=(pltpu.VMEM(x.shape, x.dtype), TOKEN),
        in_specs=[ANYWHERE] * (1 + len(tokens)),
        out_specs=(pl.BlockSpec(memory_space=pltpu.VMEM), ANYWHERE),
        scratch_shapes=[pltpu.SemaphoreType.DMA],
        compiler_params=pltpu.CompilerParams(vmem_limit_bytes=MIB),
        cost_estimate=NO_COST,
    )(pltpu.with_memory_space_constraint(x, pltpu.HBM), *tokens)


def gate_kernel(*refs):
    del refs


def gate(x, tokens):
    return pl.pallas_call(
        gate_kernel,
        out_shape=(jax.ShapeDtypeStruct(x.shape, x.dtype), TOKEN),
        in_specs=[ANYWHERE] * (1 + len(tokens)),
        out_specs=(ANYWHERE, ANYWHERE),
        input_output_aliases={0: 0},
        compiler_params=pltpu.CompilerParams(vmem_limit_bytes=MIB),
        cost_estimate=NO_COST,
    )(x, *tokens)


def product_kernel(start, has_back, tile, side_of, mine, other, weight, *refs):
    if has_back:
        back = refs[0]
        out, _, near, far, slots, in_sems, out_sems, held, back_sems = refs[-9:]
    else:
        out, _, near, far, slots, in_sems, out_sems = refs[-7:]
    many, half = near.shape
    tiles = weight.shape[1] // tile

    def back_copy(j, at):
        return pltpu.make_async_copy(back.at[:, pl.ds(at, tile)], held.at[:, pl.ds(at, tile)], back_sems.at[j])

    def out_copy(j, slot):
        at = pl.multiple_of(j * tile, tile)
        return pltpu.make_async_copy(slots.at[slot], out.at[pl.ds(start, many), pl.ds(at, tile)], out_sems.at[slot])

    fetch = [pltpu.make_async_copy(mine, near, in_sems.at[0]), pltpu.make_async_copy(other, far, in_sems.at[1])]
    for c in fetch:
        c.start()
    if has_back:
        for j in range(tiles):
            back_copy(j, j * tile).start()
    for c in fetch:
        c.wait()
    side = side_of(lax.axis_index("col"))
    near_rows = pl.ds(pl.multiple_of(side * half, half), half)
    far_rows = pl.ds(pl.multiple_of((1 - side) * half, half), half)

    def one_tile(j, carry):
        slot = lax.rem(j, 2)
        at = pl.multiple_of(j * tile, tile)
        total = jnp.dot(near[...], weight[near_rows, pl.ds(at, tile)], preferred_element_type=jnp.float32)
        total += jnp.dot(far[...], weight[far_rows, pl.ds(at, tile)], preferred_element_type=jnp.float32)
        if has_back:
            back_copy(j, at).wait()
            total += held[:, pl.ds(at, tile)]
        pl.when(j >= 2)(lambda: out_copy(j - 2, slot).wait())
        slots[slot] = total.astype(out.dtype)
        out_copy(j, slot).start()
        return carry

    lax.fori_loop(0, tiles, one_tile, 0)
    for j in range(max(0, tiles - 2), tiles):
        out_copy(j, j % 2).wait()


def product(side_of, mine, other, weight, tokens, back=None, into=None, start=0):
    depth, width = weight.shape
    many = mine.shape[0]
    tile = max(t for t in range(128, 513, 128) if width % t == 0)
    args = [mine, other, pltpu.with_memory_space_constraint(weight, pltpu.VMEM)]
    in_specs = [ANYWHERE, ANYWHERE, pl.BlockSpec(memory_space=pltpu.VMEM)]
    aliases = {}
    dtype = jnp.float32 if back is None else jnp.bfloat16
    scratch = [
        pltpu.VMEM((many, depth // 2), weight.dtype),
        pltpu.VMEM((many, depth // 2), weight.dtype),
        pltpu.VMEM((2, many, tile), dtype),
        pltpu.SemaphoreType.DMA((2,)),
        pltpu.SemaphoreType.DMA((2,)),
    ]
    total = many
    if back is not None:
        total = into[0]
        in_specs.append(ANYWHERE)
        args.append(back)
        scratch += [pltpu.VMEM((many, width), jnp.float32), pltpu.SemaphoreType.DMA((width // tile,))]
        if into[1] is not None:
            aliases = {len(args): 0}
            in_specs.append(ANYWHERE)
            args.append(into[1])
    in_specs += [ANYWHERE] * len(tokens)
    args += tokens
    return pl.pallas_call(
        functools.partial(product_kernel, start, back is not None, tile, side_of),
        out_shape=(jax.ShapeDtypeStruct((total, width), dtype), TOKEN),
        in_specs=in_specs,
        out_specs=(ANYWHERE, ANYWHERE),
        scratch_shapes=scratch,
        input_output_aliases=aliases,
        compiler_params=pltpu.CompilerParams(vmem_limit_bytes=PRODUCT_VMEM),
        cost_estimate=pl.CostEstimate(flops=4 * many * depth * width, bytes_accessed=0, transcendentals=0),
    )(*args)


def body(n_row, n_col, tokens, weight):
    inner = n_col // n_row
    assert inner == 2
    count = tokens.shape[0]
    size = count // PIECES

    def device(r, b, s):
        return (r % n_row) * n_col + (b % n_row) * inner + s

    sides = range(inner)
    chain = [(device(r, r - d, s), device(r, r - d - 1, s)) for r in range(n_row) for d in range(n_row - 1) for s in sides]
    cross = [(device(r - 1, r, s), device(r, r, s)) for r in range(n_row) for s in sides]
    everyone = [(r, b, s) for r in range(n_row) for b in range(n_row) for s in sides]
    swap_pairs = [(device(r, b, s), device(r, b, 1 - s)) for r, b, s in everyone]
    back_pairs = [(device(r, b, s), device(r - 1, b, s)) for r, b, s in everyone]

    def block_of(col):
        return lax.div(col, inner)

    def side_of(col):
        return lax.rem(col, inner)

    def distance(row, col):
        return lax.rem(row - block_of(col) + n_row, n_row)

    def crosses(row, col):
        return jnp.where(lax.rem(row + 1, n_row) == block_of(col), 0, 1)

    def sends(row, col):
        return jnp.where(row == block_of(col), 0, -1)

    tokens = pltpu.with_memory_space_constraint(tokens, pltpu.HBM)
    counts = [0, 0]
    pieces = []
    for group in STREAM:
        pieces.append((group, counts[group]))
        counts[group] += 1
    total = len(pieces)
    chunk = size // SUB
    chunks = total * SUB
    whole = SUB * (n_row + 1) - 1
    when = {at: at * SUB + whole + SUB for at, (group, _) in enumerate(pieces) if group == 1}
    sent_back = []
    for at in sorted(when):
        sent_back.append(max([when[at] + 1] + [b + BACK_STEPS for b in sent_back[-1:]]))
    for at, (group, piece) in enumerate(pieces):
        if group == 0:
            step = max(at * SUB + whole + SUB, sent_back[piece] + BACK_STEPS + 1)
            while step in when.values() or (step - whole) % SUB and step < chunks - SUB:
                step += 1
            when[at] = step

    def rows_of(k):
        return pieces[k // SUB][1] * size + k % SUB * chunk

    seen = []
    sent, held_last, mine, other, back, arriving = {}, {}, {}, {}, {}, {}
    out, waiting = None, []
    last_chain = chunks - 1 + SUB * (n_row - 1)
    first = 0 if pieces[0][0] == 1 else SUB
    for step in range(first, max(when.values()) + 1):
        if step <= last_chain + SUB:
            value, token = arriving.pop(step - SUB, None), None
            came = value
            crossing = step < chunks and pieces[step // SUB][0] == 1
            if crossing:
                options = [[tokens]] if value is None else [[tokens], [value]]
                value, token = choose(crosses, options, rows_of(step), chunk, seen)
                seen = [token]
            else:
                came = None
            if 0 <= step - SUB < chunks and pieces[step // SUB - 1][0] == 0:
                value, token = choose(sends, [[tokens]], rows_of(step - SUB), chunk, seen, value)
                seen = [token]
            if token is None:
                value, token = gate(value, seen)
                seen = [token]
            sent[step] = value
            held_last[step] = value if came is None else came
            if step <= last_chain:
                with jax.named_scope(f"chain{step}"):
                    arriving[step] = lax.ppermute(value, AXES, chain + cross if crossing else chain)
        if step == first + SUB - 1:
            weight, token = load(weight, seen)
            seen = [token]
        if waiting and step >= sent_back[waiting[0][0]]:
            piece, partial = waiting.pop(0)
            if piece > 1:
                back[piece - 2], token = gate(back[piece - 2], seen)
                seen = [token]
            partial, token = gate(partial, seen)
            seen = [token]
            with jax.named_scope(f"back{piece}"):
                back[piece] = lax.ppermute(partial, AXES, back_pairs)
        at, part = divmod(step - whole, SUB)
        if part == 0 and 0 <= at < total:
            held = [sent] * (n_row - 1) + [held_last]
            options = [[held[d][(at + 1 + d) * SUB + k] for k in range(SUB)] for d in range(n_row)]
            mine[at], token = choose(distance, options, 0, size, seen)
            seen = [token]
            with jax.named_scope(f"swap{at}"):
                other[at] = lax.ppermute(mine[at], AXES, swap_pairs)
        for at in range(total):
            if when[at] != step:
                continue
            group, piece = pieces[at]
            if group == 1:
                partial, token = product(side_of, mine[at], other[at], weight, seen)
                seen = [token]
                waiting.append((piece, partial))
            else:
                out, token = product(
                    side_of, mine[at], other[at], weight, seen, back[piece], (count, out), piece * size
                )
                seen = [token]
    return out


def solution(mesh):
    n_row, n_col = mesh.shape["row"], mesh.shape["col"]
    placed = P("row", "col")
    return jax.shard_map(
        functools.partial(body, n_row, n_col), mesh=mesh, in_specs=(placed, placed), out_specs=placed, check_vma=False
    )
```

```python
import functools

import jax
import jax.numpy as jnp
from jax import lax
from jax.experimental import pallas as pl
from jax.experimental.pallas import tpu as pltpu
from jax.sharding import PartitionSpec as P

AXES = ("row", "col")
PIECES = 8
STREAM = (0, 1, 1, 1, 1, 1, 1, 1, 1, 0, 0, 0, 0, 0, 0, 0)
SUB = 2
BACK_STEPS = 3
LOADS = 4
MIB = 1024 * 1024
CHOOSE_VMEM = 4 * MIB
PRODUCT_VMEM = 12 * MIB
ANYWHERE = pl.BlockSpec(memory_space=pl.ANY)
NO_COST = pl.CostEstimate(flops=0, bytes_accessed=0, transcendentals=0)
TOKEN = jax.ShapeDtypeStruct((8, 128), jnp.float32)


def through(sources, scratch, out, sems):
    if len(sources) == 1:
        half = out.shape[0] // 2
        sources = [sources[0].at[pl.ds(0, half)], sources[0].at[pl.ds(half, half)]]
    inward, outward, at = [], [], 0
    for i, source in enumerate(sources):
        rows = pl.ds(at, source.shape[0])
        inward.append(pltpu.make_async_copy(source, scratch.at[rows], sems.at[2 * i]))
        outward.append(pltpu.make_async_copy(scratch.at[rows], out.at[rows], sems.at[2 * i + 1]))
        at += source.shape[0]
    for c in inward:
        c.start()
    for i, c in enumerate(outward):
        inward[i].wait()
        c.start()
    for c in outward:
        c.wait()


def choose_kernel(options, parts, which_of, start, size, *refs):
    out, _, scratch, sems = refs[-4:]
    index = which_of(lax.axis_index("row"), lax.axis_index("col"))
    for value in range(options):
        sources = refs[value * parts:(value + 1) * parts]
        if parts == 1 and sources[0].shape[0] != size:
            sources = [sources[0].at[pl.ds(start, size)]]

        @pl.when(index == value)
        def _(sources=sources):
            through(sources, scratch, out, sems)


def choose(which_of, options, start, size, tokens, into=None):
    parts = len(options[0])
    width, dtype = options[0][0].shape[1], options[0][0].dtype
    args = [a for option in options for a in option] + list(tokens)
    aliases = {}
    if into is not None:
        aliases = {len(args): 0}
        args.append(into)
    return pl.pallas_call(
        functools.partial(choose_kernel, len(options), parts, which_of, start, size),
        out_shape=(jax.ShapeDtypeStruct((size, width), dtype), TOKEN),
        in_specs=[ANYWHERE] * len(args),
        out_specs=(ANYWHERE, ANYWHERE),
        scratch_shapes=[pltpu.VMEM((size, width), dtype), pltpu.SemaphoreType.DMA((2 * max(parts, 2),))],
        input_output_aliases=aliases,
        compiler_params=pltpu.CompilerParams(vmem_limit_bytes=CHOOSE_VMEM),
        cost_estimate=NO_COST,
    )(*args)


def load_kernel(start, x, *refs):
    out, _, sem = refs[-3:]
    copy = pltpu.make_async_copy(x.at[pl.ds(start, out.shape[0])], out, sem)
    copy.start()
    copy.wait()


def load(x, start, size, tokens):
    return pl.pallas_call(
        functools.partial(load_kernel, start),
        out_shape=(pltpu.VMEM((size, x.shape[1]), x.dtype), TOKEN),
        in_specs=[ANYWHERE] * (1 + len(tokens)),
        out_specs=(pl.BlockSpec(memory_space=pltpu.VMEM), ANYWHERE),
        scratch_shapes=[pltpu.SemaphoreType.DMA],
        compiler_params=pltpu.CompilerParams(vmem_limit_bytes=MIB),
        cost_estimate=NO_COST,
    )(pltpu.with_memory_space_constraint(x, pltpu.HBM), *tokens)


def gate_kernel(*refs):
    del refs


def gate(x, tokens):
    return pl.pallas_call(
        gate_kernel,
        out_shape=(jax.ShapeDtypeStruct(x.shape, x.dtype), TOKEN),
        in_specs=[ANYWHERE] * (1 + len(tokens)),
        out_specs=(ANYWHERE, ANYWHERE),
        input_output_aliases={0: 0},
        compiler_params=pltpu.CompilerParams(vmem_limit_bytes=MIB),
        cost_estimate=NO_COST,
    )(x, *tokens)


def product_kernel(start, has_back, tile, side_of, mine, other, *refs):
    weights, refs = refs[:LOADS], refs[LOADS:]
    if has_back:
        back = refs[0]
        out, _, features, slots, in_sems, out_sems, held, back_sems = refs[-8:]
    else:
        out, _, features, slots, in_sems, out_sems = refs[-6:]
    many, half = mine.shape
    part = weights[0].shape[0]
    tiles = weights[0].shape[1] // tile

    def back_copy(j, at):
        return pltpu.make_async_copy(back.at[:, pl.ds(at, tile)], held.at[:, pl.ds(at, tile)], back_sems.at[j])

    def out_copy(j, slot):
        at = pl.multiple_of(j * tile, tile)
        return pltpu.make_async_copy(slots.at[slot], out.at[pl.ds(start, many), pl.ds(at, tile)], out_sems.at[slot])

    def fetch(first, second):
        copies = [
            pltpu.make_async_copy(first, features.at[:, pl.ds(0, half)], in_sems.at[0]),
            pltpu.make_async_copy(second, features.at[:, pl.ds(half, half)], in_sems.at[1]),
        ]
        for c in copies:
            c.start()
        if has_back:
            for j in range(tiles):
                back_copy(j, j * tile).start()
        for c in copies:
            c.wait()

    side = side_of(lax.axis_index("col"))
    pl.when(side == 0)(lambda: fetch(mine, other))
    pl.when(side != 0)(lambda: fetch(other, mine))

    def one_tile(j, carry):
        slot = lax.rem(j, 2)
        at = pl.multiple_of(j * tile, tile)
        total = None
        for i, weight in enumerate(weights):
            term = jnp.dot(
                features[:, i * part:(i + 1) * part], weight[:, pl.ds(at, tile)], preferred_element_type=jnp.float32
            )
            total = term if total is None else total + term
        if has_back:
            back_copy(j, at).wait()
            total += held[:, pl.ds(at, tile)]
        pl.when(j >= 2)(lambda: out_copy(j - 2, slot).wait())
        slots[slot] = total.astype(out.dtype)
        out_copy(j, slot).start()
        return carry

    lax.fori_loop(0, tiles, one_tile, 0)
    for j in range(max(0, tiles - 2), tiles):
        out_copy(j, j % 2).wait()


def product(side_of, mine, other, weights, tokens, back=None, into=None, start=0):
    part, width = weights[0].shape
    depth = part * len(weights)
    many = mine.shape[0]
    tile = max(t for t in range(128, 513, 128) if width % t == 0)
    args = [mine, other] + [pltpu.with_memory_space_constraint(w, pltpu.VMEM) for w in weights]
    in_specs = [ANYWHERE, ANYWHERE] + [pl.BlockSpec(memory_space=pltpu.VMEM)] * len(weights)
    aliases = {}
    dtype = jnp.float32 if back is None else jnp.bfloat16
    scratch = [
        pltpu.VMEM((many, depth), mine.dtype),
        pltpu.VMEM((2, many, tile), dtype),
        pltpu.SemaphoreType.DMA((2,)),
        pltpu.SemaphoreType.DMA((2,)),
    ]
    total = many
    if back is not None:
        total = into[0]
        in_specs.append(ANYWHERE)
        args.append(back)
        scratch += [pltpu.VMEM((many, width), jnp.float32), pltpu.SemaphoreType.DMA((width // tile,))]
        if into[1] is not None:
            aliases = {len(args): 0}
            in_specs.append(ANYWHERE)
            args.append(into[1])
    in_specs += [ANYWHERE] * len(tokens)
    args += tokens
    return pl.pallas_call(
        functools.partial(product_kernel, start, back is not None, tile, side_of),
        out_shape=(jax.ShapeDtypeStruct((total, width), dtype), TOKEN),
        in_specs=in_specs,
        out_specs=(ANYWHERE, ANYWHERE),
        scratch_shapes=scratch,
        input_output_aliases=aliases,
        compiler_params=pltpu.CompilerParams(vmem_limit_bytes=PRODUCT_VMEM),
        cost_estimate=pl.CostEstimate(flops=4 * many * depth * width, bytes_accessed=0, transcendentals=0),
    )(*args)


def body(n_row, n_col, tokens, weight):
    inner = n_col // n_row
    assert inner == 2
    count = tokens.shape[0]
    size = count // PIECES

    def device(r, b, s):
        return (r % n_row) * n_col + (b % n_row) * inner + s

    sides = range(inner)
    chain = [(device(r, r - d, s), device(r, r - d - 1, s)) for r in range(n_row) for d in range(n_row - 1) for s in sides]
    cross = [(device(r - 1, r, s), device(r, r, s)) for r in range(n_row) for s in sides]
    everyone = [(r, b, s) for r in range(n_row) for b in range(n_row) for s in sides]
    swap_pairs = [(device(r, b, s), device(r, b, 1 - s)) for r, b, s in everyone]
    back_pairs = [(device(r, b, s), device(r - 1, b, s)) for r, b, s in everyone]

    def block_of(col):
        return lax.div(col, inner)

    def side_of(col):
        return lax.rem(col, inner)

    def distance(row, col):
        return lax.rem(row - block_of(col) + n_row, n_row)

    def crosses(row, col):
        return jnp.where(lax.rem(row + 1, n_row) == block_of(col), 0, 1)

    def sends(row, col):
        return jnp.where(row == block_of(col), 0, -1)

    tokens = pltpu.with_memory_space_constraint(tokens, pltpu.HBM)
    counts = [0, 0]
    pieces = []
    for group in STREAM:
        pieces.append((group, counts[group]))
        counts[group] += 1
    total = len(pieces)
    chunk = size // SUB
    chunks = total * SUB
    whole = SUB * (n_row + 1) - 1
    when = {at: at * SUB + whole + SUB for at, (group, _) in enumerate(pieces) if group == 1}
    sent_back = []
    for at in sorted(when):
        sent_back.append(max([when[at] + 1] + [b + BACK_STEPS for b in sent_back[-1:]]))
    for at, (group, piece) in enumerate(pieces):
        if group == 0:
            step = max(at * SUB + whole + SUB, sent_back[piece] + BACK_STEPS + 1)
            while step in when.values() or (step - whole) % SUB and step < chunks - SUB:
                step += 1
            when[at] = step

    def rows_of(k):
        return pieces[k // SUB][1] * size + k % SUB * chunk

    seen = []
    sent, held_last, mine, other, back, arriving = {}, {}, {}, {}, {}, {}
    out, waiting, weights = None, [], []
    last_chain = chunks - 1 + SUB * (n_row - 1)
    first = 0 if pieces[0][0] == 1 else SUB
    for step in range(first, max(when.values()) + 1):
        if step <= last_chain + SUB:
            value, token = arriving.pop(step - SUB, None), None
            came = value
            crossing = step < chunks and pieces[step // SUB][0] == 1
            if crossing:
                options = [[tokens]] if value is None else [[tokens], [value]]
                value, token = choose(crosses, options, rows_of(step), chunk, seen)
                seen = [token]
            else:
                came = None
            if 0 <= step - SUB < chunks and pieces[step // SUB - 1][0] == 0:
                value, token = choose(sends, [[tokens]], rows_of(step - SUB), chunk, seen, value)
                seen = [token]
            if token is None:
                value, token = gate(value, seen)
                seen = [token]
            sent[step] = value
            held_last[step] = value if came is None else came
            if step <= last_chain:
                with jax.named_scope(f"chain{step}"):
                    arriving[step] = lax.ppermute(value, AXES, chain + cross if crossing else chain)
        if len(weights) < LOADS and (step - first) % SUB == SUB - 1:
            part = weight.shape[0] // LOADS
            loaded, token = load(weight, len(weights) * part, part, seen)
            weights.append(loaded)
            seen = [token]
        if waiting and step >= sent_back[waiting[0][0]]:
            piece, partial = waiting.pop(0)
            if piece > 1:
                back[piece - 2], token = gate(back[piece - 2], seen)
                seen = [token]
            partial, token = gate(partial, seen)
            seen = [token]
            with jax.named_scope(f"back{piece}"):
                back[piece] = lax.ppermute(partial, AXES, back_pairs)
        at, part = divmod(step - whole, SUB)
        if part == 0 and 0 <= at < total:
            held = [sent] * (n_row - 1) + [held_last]
            options = [[held[d][(at + 1 + d) * SUB + k] for k in range(SUB)] for d in range(n_row)]
            mine[at], token = choose(distance, options, 0, size, seen)
            seen = [token]
            with jax.named_scope(f"swap{at}"):
                other[at] = lax.ppermute(mine[at], AXES, swap_pairs)
        for at in range(total):
            if when[at] != step:
                continue
            group, piece = pieces[at]
            if group == 1:
                partial, token = product(side_of, mine[at], other[at], weights, seen)
                seen = [token]
                waiting.append((piece, partial))
            else:
                out, token = product(
                    side_of, mine[at], other[at], weights, seen, back[piece], (count, out), piece * size
                )
                seen = [token]
    return out


def solution(mesh):
    n_row, n_col = mesh.shape["row"], mesh.shape["col"]
    placed = P("row", "col")
    return jax.shard_map(
        functools.partial(body, n_row, n_col), mesh=mesh, in_specs=(placed, placed), out_specs=placed, check_vma=False
    )
```

```python
import functools

import jax
import jax.numpy as jnp
from jax import lax
from jax.experimental import pallas as pl
from jax.experimental.pallas import tpu as pltpu
from jax.sharding import PartitionSpec as P

AXES = ("row", "col")
PIECES = 8
STREAM = (0, 1, 1, 1, 1, 1, 1, 1, 1, 0, 0, 0, 0, 0, 0, 0)
SUB = 2
BACK_STEPS = 3
LOADS = 4
MIB = 1024 * 1024
CHOOSE_VMEM = 4 * MIB
PRODUCT_VMEM = 12 * MIB
ANYWHERE = pl.BlockSpec(memory_space=pl.ANY)
NO_COST = pl.CostEstimate(flops=0, bytes_accessed=0, transcendentals=0)
TOKEN = jax.ShapeDtypeStruct((8, 128), jnp.float32)


def through(sources, scratch, out, sems):
    if len(sources) == 1:
        half = out.shape[0] // 2
        sources = [sources[0].at[pl.ds(0, half)], sources[0].at[pl.ds(half, half)]]
    inward, outward, at = [], [], 0
    for i, source in enumerate(sources):
        rows = pl.ds(at, source.shape[0])
        inward.append(pltpu.make_async_copy(source, scratch.at[rows], sems.at[2 * i]))
        outward.append(pltpu.make_async_copy(scratch.at[rows], out.at[rows], sems.at[2 * i + 1]))
        at += source.shape[0]
    for c in inward:
        c.start()
    for i, c in enumerate(outward):
        inward[i].wait()
        c.start()
    for c in outward:
        c.wait()


def choose_kernel(options, parts, which_of, start, size, *refs):
    out, _, scratch, sems = refs[-4:]
    index = which_of(lax.axis_index("row"), lax.axis_index("col"))
    for value in range(options):
        sources = refs[value * parts:(value + 1) * parts]
        if parts == 1 and sources[0].shape[0] != size:
            sources = [sources[0].at[pl.ds(start, size)]]

        @pl.when(index == value)
        def _(sources=sources):
            through(sources, scratch, out, sems)


def choose(which_of, options, start, size, tokens, into=None):
    parts = len(options[0])
    width, dtype = options[0][0].shape[1], options[0][0].dtype
    args = [a for option in options for a in option] + list(tokens)
    aliases = {}
    if into is not None:
        aliases = {len(args): 0}
        args.append(into)
    return pl.pallas_call(
        functools.partial(choose_kernel, len(options), parts, which_of, start, size),
        out_shape=(jax.ShapeDtypeStruct((size, width), dtype), TOKEN),
        in_specs=[ANYWHERE] * len(args),
        out_specs=(ANYWHERE, ANYWHERE),
        scratch_shapes=[pltpu.VMEM((size, width), dtype), pltpu.SemaphoreType.DMA((2 * max(parts, 2),))],
        input_output_aliases=aliases,
        compiler_params=pltpu.CompilerParams(vmem_limit_bytes=CHOOSE_VMEM),
        cost_estimate=NO_COST,
    )(*args)


def load_kernel(start, x, *refs):
    out, _, sem = refs[-3:]
    copy = pltpu.make_async_copy(x.at[pl.ds(start, out.shape[0])], out, sem)
    copy.start()
    copy.wait()


def load(x, start, size, tokens):
    return pl.pallas_call(
        functools.partial(load_kernel, start),
        out_shape=(pltpu.VMEM((size, x.shape[1]), x.dtype), TOKEN),
        in_specs=[ANYWHERE] * (1 + len(tokens)),
        out_specs=(pl.BlockSpec(memory_space=pltpu.VMEM), ANYWHERE),
        scratch_shapes=[pltpu.SemaphoreType.DMA],
        compiler_params=pltpu.CompilerParams(vmem_limit_bytes=MIB),
        cost_estimate=NO_COST,
    )(pltpu.with_memory_space_constraint(x, pltpu.HBM), *tokens)


def gate_kernel(*refs):
    del refs


def gate(x, tokens):
    return pl.pallas_call(
        gate_kernel,
        out_shape=(jax.ShapeDtypeStruct(x.shape, x.dtype), TOKEN),
        in_specs=[ANYWHERE] * (1 + len(tokens)),
        out_specs=(ANYWHERE, ANYWHERE),
        input_output_aliases={0: 0},
        compiler_params=pltpu.CompilerParams(vmem_limit_bytes=MIB),
        cost_estimate=NO_COST,
    )(x, *tokens)


def product_kernel(start, has_back, tile, side_of, mine, other, *refs):
    weights, refs = refs[:LOADS], refs[LOADS:]
    if has_back:
        back = refs[0]
        out, _, features, slots, in_sems, out_sems, held, back_sems = refs[-8:]
    else:
        out, _, features, slots, in_sems, out_sems = refs[-6:]
    many, half = mine.shape
    part = weights[0].shape[0]
    tiles = weights[0].shape[1] // tile

    def back_copy(j, at):
        return pltpu.make_async_copy(back.at[:, pl.ds(at, tile)], held.at[:, pl.ds(at, tile)], back_sems.at[j])

    def out_copy(j, slot):
        at = pl.multiple_of(j * tile, tile)
        return pltpu.make_async_copy(slots.at[slot], out.at[pl.ds(start, many), pl.ds(at, tile)], out_sems.at[slot])

    def fetch(first, second):
        copies = [
            pltpu.make_async_copy(first, features.at[:, pl.ds(0, half)], in_sems.at[0]),
            pltpu.make_async_copy(second, features.at[:, pl.ds(half, half)], in_sems.at[1]),
        ]
        for c in copies:
            c.start()
        if has_back:
            for j in range(tiles):
                back_copy(j, j * tile).start()
        for c in copies:
            c.wait()

    side = side_of(lax.axis_index("col"))
    pl.when(side == 0)(lambda: fetch(mine, other))
    pl.when(side != 0)(lambda: fetch(other, mine))

    def one_tile(j, carry):
        slot = lax.rem(j, 2)
        at = pl.multiple_of(j * tile, tile)
        total = None
        for i, weight in enumerate(weights):
            term = jnp.dot(
                features[:, i * part:(i + 1) * part], weight[:, pl.ds(at, tile)], preferred_element_type=jnp.float32
            )
            total = term if total is None else total + term
        if has_back:
            back_copy(j, at).wait()
            total += held[:, pl.ds(at, tile)]
        pl.when(j >= 2)(lambda: out_copy(j - 2, slot).wait())
        slots[slot] = total.astype(out.dtype)
        out_copy(j, slot).start()
        return carry

    lax.fori_loop(0, tiles, one_tile, 0)
    for j in range(max(0, tiles - 2), tiles):
        out_copy(j, j % 2).wait()


def product(side_of, mine, other, weights, tokens, back=None, into=None, start=0):
    part, width = weights[0].shape
    depth = part * len(weights)
    many = mine.shape[0]
    tile = max(t for t in range(128, 513, 128) if width % t == 0)
    args = [mine, other] + [pltpu.with_memory_space_constraint(w, pltpu.VMEM) for w in weights]
    in_specs = [ANYWHERE, ANYWHERE] + [pl.BlockSpec(memory_space=pltpu.VMEM)] * len(weights)
    aliases = {}
    dtype = jnp.float32 if back is None else jnp.bfloat16
    scratch = [
        pltpu.VMEM((many, depth), mine.dtype),
        pltpu.VMEM((2, many, tile), dtype),
        pltpu.SemaphoreType.DMA((2,)),
        pltpu.SemaphoreType.DMA((2,)),
    ]
    total = many
    if back is not None:
        total = into[0]
        in_specs.append(ANYWHERE)
        args.append(back)
        scratch += [pltpu.VMEM((many, width), jnp.float32), pltpu.SemaphoreType.DMA((width // tile,))]
        if into[1] is not None:
            aliases = {len(args): 0}
            in_specs.append(ANYWHERE)
            args.append(into[1])
    in_specs += [ANYWHERE] * len(tokens)
    args += tokens
    return pl.pallas_call(
        functools.partial(product_kernel, start, back is not None, tile, side_of),
        out_shape=(jax.ShapeDtypeStruct((total, width), dtype), TOKEN),
        in_specs=in_specs,
        out_specs=(ANYWHERE, ANYWHERE),
        scratch_shapes=scratch,
        input_output_aliases=aliases,
        compiler_params=pltpu.CompilerParams(vmem_limit_bytes=PRODUCT_VMEM),
        cost_estimate=pl.CostEstimate(flops=8 * many * depth * width, bytes_accessed=0, transcendentals=0),
    )(*args)


def body(n_row, n_col, tokens, weight):
    inner = n_col // n_row
    assert inner == 2
    count = tokens.shape[0]
    size = count // PIECES

    def device(r, b, s):
        return (r % n_row) * n_col + (b % n_row) * inner + s

    sides = range(inner)
    chain = [(device(r, r - d, s), device(r, r - d - 1, s)) for r in range(n_row) for d in range(n_row - 1) for s in sides]
    cross = [(device(r - 1, r, s), device(r, r, s)) for r in range(n_row) for s in sides]
    everyone = [(r, b, s) for r in range(n_row) for b in range(n_row) for s in sides]
    swap_pairs = [(device(r, b, s), device(r, b, 1 - s)) for r, b, s in everyone]
    back_pairs = [(device(r, b, s), device(r - 1, b, s)) for r, b, s in everyone]

    def block_of(col):
        return lax.div(col, inner)

    def side_of(col):
        return lax.rem(col, inner)

    def distance(row, col):
        return lax.rem(row - block_of(col) + n_row, n_row)

    def crosses(row, col):
        return jnp.where(lax.rem(row + 1, n_row) == block_of(col), 0, 1)

    def sends(row, col):
        return jnp.where(row == block_of(col), 0, -1)

    tokens = pltpu.with_memory_space_constraint(tokens, pltpu.HBM)
    counts = [0, 0]
    pieces = []
    for group in STREAM:
        pieces.append((group, counts[group]))
        counts[group] += 1
    total = len(pieces)
    chunk = size // SUB
    chunks = total * SUB
    whole = SUB * (n_row + 1) - 1
    when = {at: at * SUB + whole + SUB for at, (group, _) in enumerate(pieces) if group == 1}
    sent_back = []
    for at in sorted(when):
        sent_back.append(max([when[at] + 1] + [b + BACK_STEPS for b in sent_back[-1:]]))
    for at, (group, piece) in enumerate(pieces):
        if group == 0:
            step = max(at * SUB + whole + SUB, sent_back[piece] + BACK_STEPS + 1)
            while step in when.values() or (step - whole) % SUB and step < chunks - SUB:
                step += 1
            when[at] = step

    def rows_of(k):
        return pieces[k // SUB][1] * size + k % SUB * chunk

    seen = []
    sent, held_last, mine, other, back, arriving = {}, {}, {}, {}, {}, {}
    out, waiting, weights = None, [], []
    last_chain = chunks - 1 + SUB * (n_row - 1)
    first = 0 if pieces[0][0] == 1 else SUB
    for step in range(first, max(when.values()) + 1):
        if step <= last_chain + SUB:
            value, token = arriving.pop(step - SUB, None), None
            came = value
            crossing = step < chunks and pieces[step // SUB][0] == 1
            if crossing:
                options = [[tokens]] if value is None else [[tokens], [value]]
                value, token = choose(crosses, options, rows_of(step), chunk, seen)
                seen = [token]
            else:
                came = None
            if 0 <= step - SUB < chunks and pieces[step // SUB - 1][0] == 0:
                value, token = choose(sends, [[tokens]], rows_of(step - SUB), chunk, seen, value)
                seen = [token]
            if token is None:
                value, token = gate(value, seen)
                seen = [token]
            sent[step] = value
            held_last[step] = value if came is None else came
            if step <= last_chain:
                with jax.named_scope(f"chain{step}"):
                    arriving[step] = lax.ppermute(value, AXES, chain + cross if crossing else chain)
        if len(weights) < LOADS and (step - first) % SUB == SUB - 1:
            part = weight.shape[0] // LOADS
            loaded, token = load(weight, len(weights) * part, part, seen)
            weights.append(loaded)
            seen = [token]
        if waiting and step >= sent_back[waiting[0][0]]:
            piece, partial = waiting.pop(0)
            if piece > 1:
                back[piece - 2], token = gate(back[piece - 2], seen)
                seen = [token]
            partial, token = gate(partial, seen)
            seen = [token]
            with jax.named_scope(f"back{piece}"):
                back[piece] = lax.ppermute(partial, AXES, back_pairs)
        at, part = divmod(step - whole, SUB)
        if part == 0 and 0 <= at < total:
            held = [sent] * (n_row - 1) + [held_last]
            options = [[held[d][(at + 1 + d) * SUB + k] for k in range(SUB)] for d in range(n_row)]
            mine[at], token = choose(distance, options, 0, size, seen)
            seen = [token]
            with jax.named_scope(f"swap{at}"):
                other[at] = lax.ppermute(mine[at], AXES, swap_pairs)
        for at in range(total):
            if when[at] != step:
                continue
            group, piece = pieces[at]
            if group == 1:
                partial, token = product(side_of, mine[at], other[at], weights, seen)
                seen = [token]
                waiting.append((piece, partial))
            else:
                out, token = product(
                    side_of, mine[at], other[at], weights, seen, back[piece], (count, out), piece * size
                )
                seen = [token]
    return out


def solution(mesh):
    n_row, n_col = mesh.shape["row"], mesh.shape["col"]
    placed = P("row", "col")
    return jax.shard_map(
        functools.partial(body, n_row, n_col), mesh=mesh, in_specs=(placed, placed), out_specs=placed, check_vma=False
    )
```
